32 devices in a mesh: dp: 4 (over x, core), ctx: 8 (over z, y).
Axes of the slice: x: 2, y: 2, z: 4, core: 2. Of those that a mesh axis runs over, the one named last changes fastest.
Arguments:
- hidden: bfloat16 [4, 2048, 8192], P('dp', 'ctx')
- norm_gain: bfloat16 [8192], replicated, may hold values from 0.5 to 2
- queries: bfloat16 [4, 2048, 4096], P('dp', 'ctx')
- key_weight: bfloat16 [8192, 512], P('dp'), may hold values from -0.0625 to 0.0625
- value_weight: bfloat16 [8192, 512], P('dp'), may hold values from -0.0625 to 0.0625
- block_lists: int32 [4, 32, 16, 12], P('dp', 'ctx'), may hold values from 0 to 15, as said below
- block_counts: int32 [4, 32, 16], P('dp', 'ctx'), may hold values from 1 to 12, as said below
Outputs:
- attended: bfloat16 [4, 2048, 4096], P('dp', 'ctx')
The draws below stay inside these ranges and needn't reach their ends.
Inputs may be any that keep to these rules, and one draw needn't show every extreme that they name: `block_lists`: for each spreadsheet, head and query block i, the first block_counts entries are distinct key blocks: the first is i, each later one is smaller than the one before (the blocks of i's ancestors in that head's header tree, nearest first); entries past the count equal i and are to be ignored. `block_counts`: every spreadsheet has a query block with 12 listed blocks; the counts differ much from head to head.
All inputs are finite; a program needn't handle non-finite values.
Results may differ from the reference program's by a relative error of at most 0.0078.
Values may be sent and summed in bfloat16 or wider, within the bound.
A program may use at most 128 MiB of HBM per device.

```python
import math
import jax
import jax.numpy as jnp
from jax import lax

D = 8192
QH = 32
KVH = 4
HD = 128
BLK = 128
MAXB = 12
BATCH = 4
SEQ = 2048
NB = 16


def draw_hidden(key, part):
    first, second, third = jax.random.split(key, 3)
    row_scale = jnp.exp(jax.random.uniform(second, (BATCH, SEQ, 1), minval=0.0, maxval=math.log(10.0)))
    col_scale = jnp.exp(jax.random.uniform(third, (D,), minval=0.0, maxval=math.log(10.0)))
    base = jax.random.normal(first, (BATCH, SEQ, D))
    return (base * row_scale * col_scale).astype(jnp.bfloat16)


def draw_queries(key, part):
    first = jax.random.fold_in(key, 0)
    base = jax.random.normal(first, (BATCH, SEQ, QH * HD))
    return base.astype(jnp.bfloat16)


def ancestry(key):
    key_thr, key_coin, key_far, key_head, key_start = jax.random.split(key, 5)
    blocks = jnp.arange(NB, dtype=jnp.int32)
    threshold = jax.random.randint(key_thr, (BATCH, QH, 1), 1, 10)
    coins = jax.random.randint(key_coin, (BATCH, QH, NB), 0, 10)
    far_parent = jax.random.randint(key_far, (BATCH, QH, NB), 0, jnp.maximum(blocks, 1))
    parent = jnp.maximum(jnp.where(coins < threshold, blocks - 1, far_parent), 0)
    forced_head = jax.random.randint(key_head, (BATCH, 1, 1), 0, QH)
    chain_end = jax.random.randint(key_start, (BATCH, 1, 1), MAXB - 1, NB)
    in_chain = (jnp.arange(QH)[None, :, None] == forced_head) & (blocks > chain_end - MAXB + 1) & (blocks <= chain_end)
    parent = jnp.where(in_chain, blocks - 1, parent).astype(jnp.int32)
    current = jnp.broadcast_to(blocks, (BATCH, QH, NB))
    entries = [current]
    alive = current != 0
    counted = jnp.ones((BATCH, QH, NB), jnp.int32)
    for step_index in range(MAXB - 1):
        following = jnp.take_along_axis(parent, current, axis=2)
        entries.append(jnp.where(alive, following, blocks))
        counted = counted + alive.astype(jnp.int32)
        alive = alive & (following != 0)
        current = following
    return (jnp.stack(entries, axis=-1).astype(jnp.int32), counted.astype(jnp.int32))


def draw_block_lists(key, part):
    return ancestry(jax.random.fold_in(key, 11))[0]


def draw_block_counts(key, part):
    return ancestry(jax.random.fold_in(key, 11))[1]


def shard_levels(own_key, extent, shards, least, largest):
    gain, own = 1.0, jax.random.fold_in(own_key, 6)
    for axis_at, parts in shards:
        heights = jnp.exp(jax.random.uniform(jax.random.fold_in(own, axis_at), (parts,), jnp.float32, least / len(shards), largest / len(shards)))
        gain = gain * jnp.repeat(heights, extent[axis_at] // parts).reshape([-1 if axis == axis_at else 1 for axis in range(len(extent))])
    return gain


def bell_draw(own_key, shape, scale, most, cuts=(), kind=jnp.bfloat16):
    gain = shard_levels(own_key, shape, cuts, -0.22, 0.18) if cuts else 1.0
    values = jax.random.normal(own_key, shape, jnp.float32) * scale * gain
    return jnp.minimum(jnp.maximum(values, -most), most).astype(kind)


def setup_inputs(seed: int = 0) -> dict:
    splits = jax.random.split(jax.random.key(seed), 8)
    hidden = draw_hidden(jax.random.fold_in(splits[7], 71), 0)
    norm_gain = jnp.clip(jnp.exp(jax.random.uniform(splits[1], (D,), jnp.float32, math.log(0.5), math.log(2.0))), 0.5, 2.0).astype(jnp.bfloat16)
    queries = draw_queries(jax.random.fold_in(splits[7], 71), 0)
    key_weight = bell_draw(splits[3], (D, KVH * HD), D ** -0.5, 0.0625, ((0, 4),))
    value_weight = bell_draw(splits[4], (D, KVH * HD), D ** -0.5, 0.0625, ((0, 4),))
    block_lists = draw_block_lists(jax.random.fold_in(splits[7], 71), 0)
    block_counts = draw_block_counts(jax.random.fold_in(splits[7], 71), 0)
    return dict(hidden=hidden, norm_gain=norm_gain, queries=queries, key_weight=key_weight, value_weight=value_weight, block_lists=block_lists, block_counts=block_counts)


def attend_head(bundle):
    query_head, key_head, value_head, lists_one, counts_one = bundle
    score_scale = HD ** (-0.5)
    query_tiles = query_head.reshape(NB, BLK, HD).astype(jnp.float32)
    key_tiles = jnp.take(key_head.reshape(NB, BLK, HD), lists_one, axis=0).astype(jnp.float32)
    value_tiles = jnp.take(value_head.reshape(NB, BLK, HD), lists_one, axis=0).astype(jnp.float32)
    scores = jnp.einsum('ntd,nskd->ntsk', query_tiles, key_tiles) * score_scale
    slot_ids = jnp.arange(MAXB)
    live_slots = slot_ids[None, :] < counts_one[:, None]
    causal = (slot_ids[None, :, None] > 0) | (jnp.arange(BLK)[None, None, :] <= jnp.arange(BLK)[:, None, None])
    allowed = live_slots[:, None, :, None] & causal[None]
    masked = jnp.where(allowed, scores, -jnp.inf)
    row_peak = lax.optimization_barrier(jnp.max(masked, axis=(2, 3), keepdims=True))
    exponent = jnp.exp(masked - row_peak)
    denominator = lax.optimization_barrier(jnp.sum(exponent, axis=(2, 3)))
    rounded = lax.optimization_barrier(exponent.astype(jnp.bfloat16)).astype(jnp.float32)
    weighted = jnp.einsum('ntsk,nskd->ntd', rounded, value_tiles)
    return (weighted / denominator[..., None]).astype(jnp.bfloat16).reshape(SEQ, HD)

def reference(hidden, norm_gain, queries, key_weight, value_weight, block_lists, block_counts):
    upcast = hidden.astype(jnp.float32)
    mean_square = lax.optimization_barrier(jnp.mean(upcast * upcast, axis=-1, keepdims=True))
    normed = (upcast * lax.rsqrt(mean_square + 1e-05) * norm_gain.astype(jnp.float32)).astype(jnp.bfloat16)
    flat_rows = normed.reshape(BATCH * SEQ, D)
    keys_all = jnp.dot(flat_rows, key_weight, preferred_element_type=jnp.float32).astype(jnp.bfloat16)
    values_all = jnp.dot(flat_rows, value_weight, preferred_element_type=jnp.float32).astype(jnp.bfloat16)
    group_size = QH // KVH
    key_heads = jnp.repeat(jnp.transpose(keys_all.reshape(BATCH, SEQ, KVH, HD), (0, 2, 1, 3)), group_size, axis=1).reshape(BATCH * QH, SEQ, HD)
    value_heads = jnp.repeat(jnp.transpose(values_all.reshape(BATCH, SEQ, KVH, HD), (0, 2, 1, 3)), group_size, axis=1).reshape(BATCH * QH, SEQ, HD)
    query_heads = jnp.transpose(queries.reshape(BATCH, SEQ, QH, HD), (0, 2, 1, 3)).reshape(BATCH * QH, SEQ, HD)
    lists_flat = block_lists.reshape(BATCH * QH, NB, MAXB)
    counts_flat = block_counts.reshape(BATCH * QH, NB)
    results = lax.map(attend_head, (query_heads, key_heads, value_heads, lists_flat, counts_flat))
    return jnp.transpose(results.reshape(BATCH, QH, SEQ, HD), (0, 2, 1, 3)).reshape(BATCH, SEQ, QH * HD)
```

```python
import functools

import jax
import jax.numpy as jnp
from jax import lax
from jax.experimental import pallas as pl
from jax.experimental.pallas import tpu as pltpu
from jax.sharding import PartitionSpec as P

KVH = 4
HD = 128
BLK = 128
MAXB = 12
LOG2E = 1.4426950408889634
BUCKETS = (2, 4, 6, 8, 10, 12)


def attention_kernel(heads, local_blocks, lists_ref, queries_ref, pairs_ref, out_ref):
    group = heads // KVH
    width = MAXB + 1
    factor = LOG2E * HD ** (-0.5)

    def one(index, carry):
        block = index // heads
        head = lax.rem(index, heads)
        kv = head // group
        base = (head * local_blocks + block) * width
        count = lists_ref[base + MAXB]
        rows = pl.ds(pl.multiple_of(block * BLK, BLK), BLK)
        columns = pl.ds(pl.multiple_of(head * HD, HD), HD)
        key_columns = pl.ds(pl.multiple_of(kv * HD, HD), HD)
        value_columns = pl.ds(pl.multiple_of((KVH + kv) * HD, HD), HD)

        def attend(slots):
            query = queries_ref[rows, columns]
            places = [
                pl.ds(pl.multiple_of(lists_ref[base + s] * BLK, BLK), BLK) for s in range(slots)
            ]
            keys = jnp.concatenate([pairs_ref[place, key_columns] for place in places], axis=0)
            scores = lax.dot_general(
                query, keys, (((1,), (1,)), ((), ())), preferred_element_type=jnp.float32
            )
            tiles = [scores[:, s * BLK : (s + 1) * BLK] for s in range(slots)]
            row = lax.broadcasted_iota(jnp.int32, (BLK, BLK), 0)
            column = lax.broadcasted_iota(jnp.int32, (BLK, BLK), 1)
            tiles[0] = jnp.where(column <= row, tiles[0], -jnp.inf)
            for s in range(max(1, slots - 1), slots):
                tiles[s] = jnp.where(s < count, tiles[s], -jnp.inf)
            peak = functools.reduce(jnp.maximum, tiles)
            peak = jnp.max(peak, axis=1, keepdims=True)
            tiles = [jnp.exp2((tile - peak) * factor) for tile in tiles]
            total = jnp.sum(functools.reduce(jnp.add, tiles), axis=1, keepdims=True)
            weights = jnp.concatenate([tile.astype(jnp.bfloat16) for tile in tiles], axis=1)
            values = jnp.concatenate([pairs_ref[place, value_columns] for place in places], axis=0)
            attended = jnp.dot(weights, values, preferred_element_type=jnp.float32)
            out_ref[rows, columns] = (attended / total).astype(jnp.bfloat16)

        below = 0
        for slots in BUCKETS:

            @pl.when((count > below) & (count <= slots))
            def _(slots=slots):
                attend(slots)

            below = slots
        return carry

    lax.fori_loop(0, heads * local_blocks, one, 0)


def attention(lists, queries, pairs, heads, local_blocks):
    return pl.pallas_call(
        functools.partial(attention_kernel, heads, local_blocks),
        out_shape=jax.ShapeDtypeStruct(queries.shape, jnp.bfloat16),
        in_specs=[
            pl.BlockSpec(memory_space=pltpu.SMEM),
            pl.BlockSpec(memory_space=pltpu.VMEM),
            pl.BlockSpec(memory_space=pltpu.VMEM),
        ],
        out_specs=pl.BlockSpec(memory_space=pltpu.VMEM),
        compiler_params=pltpu.CompilerParams(vmem_limit_bytes=48 * 2**20),
    )(lists, queries, pairs)


def on_device(hidden, norm_gain, queries, key_weight, value_weight, block_lists, block_counts):
    tables = jnp.concatenate([block_lists[0], block_counts[0][..., None]], axis=-1)
    tables = lax.all_to_all(tables, "ctx", split_axis=1, concat_axis=0, tiled=True)
    heads, local_blocks, _ = tables.shape
    upcast = hidden[0].astype(jnp.float32)
    mean_square = jnp.mean(upcast * upcast, axis=-1, keepdims=True)
    normed = (upcast * lax.rsqrt(mean_square + 1e-05) * norm_gain.astype(jnp.float32)).astype(
        jnp.bfloat16
    )
    key_all = lax.all_gather(key_weight, "dp", axis=0, tiled=True)
    value_all = lax.all_gather(value_weight, "dp", axis=0, tiled=True)
    keys = jnp.dot(normed, key_all, preferred_element_type=jnp.float32).astype(jnp.bfloat16)
    values = jnp.dot(normed, value_all, preferred_element_type=jnp.float32).astype(jnp.bfloat16)
    pairs = lax.all_gather(jnp.concatenate([keys, values], axis=1), "ctx", axis=0, tiled=True)
    return attention(tables.reshape(-1), queries[0], pairs, heads, local_blocks)[None]


def solution(mesh):
    return jax.shard_map(
        on_device,
        mesh=mesh,
        in_specs=(
            P("dp", "ctx", None),
            P(),
            P("dp", "ctx", None),
            P("dp", None),
            P("dp", None),
            P("dp", "ctx", None, None),
            P("dp", "ctx", None),
        ),
        out_specs=P("dp", "ctx", None),
        check_vma=False,
    )
```

```python
import functools

import jax
import jax.numpy as jnp
from jax import lax
from jax.experimental import pallas as pl
from jax.experimental.pallas import tpu as pltpu
from jax.sharding import PartitionSpec as P

KVH = 4
HD = 128
BLK = 128
MAXB = 12
LOG2E = 1.4426950408889634
PIECES = 4
MESH = pl.DeviceIdType.MESH
BUCKETS = (2, 4, 6, 8, 10, 12)


def attention_kernel(heads, local_blocks, lists_ref, queries_ref, pairs_ref, out_ref):
    group = heads // KVH
    heads_each = heads // lists_ref.shape[0]
    factor = LOG2E * HD ** (-0.5)

    def one(index, carry):
        block = index // heads
        head = lax.rem(index, heads)
        kv = head // group
        source = head // heads_each
        entry = lax.rem(head, heads_each) * local_blocks + block
        count = lists_ref[source, entry, MAXB]
        rows = pl.ds(pl.multiple_of(block * BLK, BLK), BLK)
        columns = pl.ds(pl.multiple_of(head * HD, HD), HD)
        key_columns = pl.ds(pl.multiple_of(kv * HD, HD), HD)

        def attend(slots):
            query = queries_ref[rows, columns]
            chosen = [lists_ref[source, entry, s] for s in range(slots)]
            places = [
                (
                    pick // local_blocks,
                    pl.ds(pl.multiple_of(lax.rem(pick, local_blocks) * BLK, BLK), BLK),
                )
                for pick in chosen
            ]
            keys = jnp.concatenate(
                [pairs_ref[owner, 0, place, key_columns] for owner, place in places], axis=0
            )
            scores = lax.dot_general(
                query, keys, (((1,), (1,)), ((), ())), preferred_element_type=jnp.float32
            )
            tiles = [scores[:, s * BLK : (s + 1) * BLK] for s in range(slots)]
            row = lax.broadcasted_iota(jnp.int32, (BLK, BLK), 0)
            column = lax.broadcasted_iota(jnp.int32, (BLK, BLK), 1)
            tiles[0] = jnp.where(column <= row, tiles[0], -jnp.inf)
            for s in range(max(1, slots - 1), slots):
                tiles[s] = jnp.where(s < count, tiles[s], -jnp.inf)
            peak = functools.reduce(jnp.maximum, tiles)
            peak = jnp.max(peak, axis=1, keepdims=True)
            tiles = [jnp.exp2((tile - peak) * factor) for tile in tiles]
            total = jnp.sum(functools.reduce(jnp.add, tiles), axis=1, keepdims=True)
            weights = jnp.concatenate([tile.astype(jnp.bfloat16) for tile in tiles], axis=1)
            values = jnp.concatenate(
                [pairs_ref[owner, 1, place, key_columns] for owner, place in places], axis=0
            )
            attended = jnp.dot(weights, values, preferred_element_type=jnp.float32)
            out_ref[rows, columns] = (attended / total).astype(jnp.bfloat16)

        below = 0
        for slots in BUCKETS:

            @pl.when((count > below) & (count <= slots))
            def _(slots=slots):
                attend(slots)

            below = slots
        return carry

    lax.fori_loop(0, heads * local_blocks, one, 0)


def attention(lists, queries, pairs, heads, local_blocks):
    return pl.pallas_call(
        functools.partial(attention_kernel, heads, local_blocks),
        out_shape=jax.ShapeDtypeStruct(queries.shape, jnp.bfloat16),
        in_specs=[
            pl.BlockSpec(memory_space=pltpu.SMEM),
            pl.BlockSpec(memory_space=pltpu.VMEM),
            pl.BlockSpec(memory_space=pltpu.VMEM),
        ],
        out_specs=pl.BlockSpec(memory_space=pltpu.VMEM),
        compiler_params=pltpu.CompilerParams(vmem_limit_bytes=48 * 2**20),
    )(lists, queries, pairs)


def gather_kernel(
    ctx_size,
    hidden_ref,
    gain_ref,
    key_ref,
    value_ref,
    table_ref,
    pairs_ref,
    tables_ref,
    weights,
    rows_in,
    normed,
    totals,
    own_pair,
    x_sems,
    y_sems,
    core_sems,
    core_x_sems,
    core_y_sems,
    ring_sems,
    table_sems,
    local_sems,
):
    dp = lax.axis_index("dp")
    ctx = lax.axis_index("ctx")
    core = dp % 2
    core_peer = dp + 1 - 2 * core
    x_peer = dp + 2 - 4 * (dp // 2)
    cross_peer = x_peer + 1 - 2 * core
    side = ctx % 2
    y_peer = ctx + 1 - 2 * side
    half_ring = ctx_size // 2
    position = (1 - side) * (ctx // 2) + side * (ctx_size - 1 - ctx // 2)

    def ctx_at(place):
        place = (place + ctx_size) % ctx_size
        second = place // half_ring
        return (1 - second) * 2 * place + second * (2 * (ctx_size - 1 - place) + 1)

    shard = key_ref.shape[0]
    half = shard // 2
    chunk = half // PIECES
    sources = (key_ref, value_ref)
    total_pieces = 2 * PIECES

    barrier = pltpu.get_barrier_semaphore()
    for step in range(1, ctx_size):
        pl.semaphore_signal(
            barrier, inc=1, device_id={"ctx": (ctx + step) % ctx_size}, device_id_type=MESH
        )
    for peer in (core_peer, x_peer):
        pl.semaphore_signal(barrier, inc=1, device_id={"dp": peer}, device_id_type=MESH)
    pl.semaphore_wait(barrier, ctx_size + 1)

    def remote(src, dst, sems, index, device):
        return pltpu.make_async_remote_copy(
            src_ref=src,
            dst_ref=dst,
            send_sem=sems.at[(0, *index)],
            recv_sem=sems.at[(1, *index)],
            device_id=device,
            device_id_type=MESH,
        )

    def piece_rows(which, k):
        return pl.ds(pl.multiple_of(which * half + (k % PIECES) * chunk, chunk), chunk)

    x_copies, y_copies, core_copies, core_x, core_y, own_copies = [], [], [], [], [], []
    for k in range(total_pieces):
        j = k // PIECES
        mine, other = piece_rows(side, k), piece_rows(1 - side, k)
        quarter = pl.ds((k % PIECES) * 2 * chunk, 2 * chunk)
        x_copies.append(
            remote(sources[j].at[mine], weights.at[dp, j, mine], x_sems, (k,), {"dp": x_peer})
        )
        arrived = weights.at[x_peer, j, mine]
        y_copies.append(remote(arrived, arrived, y_sems, (k,), {"ctx": y_peer}))
        core_x.append(remote(arrived, arrived, core_x_sems, (k,), {"dp": core_peer}))
        second = weights.at[x_peer, j, other]
        core_y.append(remote(second, second, core_y_sems, (k,), {"dp": core_peer}))
        core_copies.append(
            remote(
                sources[j].at[quarter],
                weights.at[dp, j, quarter],
                core_sems,
                (k,),
                {"dp": core_peer},
            )
        )
        own_copies.append(
            pltpu.make_async_copy(
                sources[j].at[quarter], weights.at[dp, j, quarter], local_sems.at[k]
            )
        )

    load = pltpu.make_async_copy(hidden_ref, rows_in, local_sems.at[total_pieces])
    load.start()
    for k in range(total_pieces):
        x_copies[k].start()
    for k in range(total_pieces):
        core_copies[k].start()
        own_copies[k].start()
    own_table = pltpu.make_async_copy(
        table_ref.at[ctx], tables_ref.at[ctx], local_sems.at[total_pieces + 1]
    )
    own_table.start()
    table_copies = []
    for step in range(1, ctx_size):
        to = (ctx + step) % ctx_size
        table_copies.append(
            remote(table_ref.at[to], tables_ref.at[ctx], table_sems, (step,), {"ctx": to})
        )
        table_copies[-1].start()

    totals[...] = jnp.zeros_like(totals)
    load.wait()
    strip = 16

    @pl.loop(0, rows_in.shape[0] // strip)
    def _(index):
        rows = pl.ds(pl.multiple_of(index * strip, strip), strip)
        upcast = rows_in[rows, :].astype(jnp.float32)
        mean_square = jnp.mean(upcast * upcast, axis=-1, keepdims=True)
        gain = gain_ref[...].astype(jnp.float32)
        normed[rows, :] = (upcast * lax.rsqrt(mean_square + 1e-05) * gain).astype(jnp.bfloat16)

    def accumulate(owner, j, start, size):
        columns = pl.ds(pl.multiple_of(owner * shard + start, chunk), size)
        totals[j] += jnp.dot(
            normed[:, columns],
            weights[owner, j, pl.ds(pl.multiple_of(start, chunk), size), :],
            preferred_element_type=jnp.float32,
        )

    def ring_copy(j, way, step):
        sign = 1 - 2 * way
        origin = ctx_at(position - sign * step)
        source = own_pair.at[j] if step == 0 else pairs_ref.at[origin, j]
        return remote(
            source,
            pairs_ref.at[origin, j],
            ring_sems,
            (j, way, step),
            {"ctx": ctx_at(position + sign)},
        )

    def hops(j, way):
        return half_ring if j == way else half_ring - 1

    sent, own_stores = [], []

    def ring_start(j, step):
        for way in range(2):
            if step < hops(j, way):
                copy = ring_copy(j, way, step)
                copy.start()
                sent.append(copy)

    def ring_wait(j, step):
        for way in range(2):
            if step < hops(j, way):
                ring_copy(j, way, step).wait_recv()

    def finish(j):
        own_pair[j] = totals[j].astype(jnp.bfloat16)
        store = pltpu.make_async_copy(
            own_pair.at[j], pairs_ref.at[ctx, j], local_sems.at[total_pieces + 2 + j]
        )
        store.start()
        own_stores.append(store)
        ring_start(j, 0)

    key_step = 0
    for k in range(total_pieces + 2):
        if k < total_pieces:
            x_copies[k].wait_recv()
            y_copies[k].start()
            core_x[k].start()
        if 1 <= k <= total_pieces:
            y_copies[k - 1].wait_recv()
            core_y[k - 1].start()
        if k < total_pieces:
            j, at = k // PIECES, (k % PIECES) * chunk
            own_copies[k].wait()
            accumulate(dp, j, 2 * at, 2 * chunk)
            core_copies[k].wait_recv()
            accumulate(core_peer, j, 2 * at, 2 * chunk)
            accumulate(x_peer, j, side * half + at, chunk)
        if 1 <= k <= total_pieces:
            j, at = (k - 1) // PIECES, ((k - 1) % PIECES) * chunk
            accumulate(x_peer, j, (1 - side) * half + at, chunk)
            core_x[k - 1].wait_recv()
            accumulate(cross_peer, j, side * half + at, chunk)
        if 2 <= k:
            j, at = (k - 2) // PIECES, ((k - 2) % PIECES) * chunk
            core_y[k - 2].wait_recv()
            accumulate(cross_peer, j, (1 - side) * half + at, chunk)
        if k == PIECES + 1:
            finish(0)
        if k > PIECES + 1 and key_step < half_ring - 1:
            ring_wait(0, key_step)
            key_step += 1
            ring_start(0, key_step)
    finish(1)
    value_step = 0
    while key_step < half_ring or value_step < half_ring:
        for j, step in ((0, key_step), (1, value_step)):
            if step < half_ring:
                ring_wait(j, step)
                if step + 1 < half_ring:
                    ring_start(j, step + 1)
        key_step, value_step = min(key_step + 1, half_ring), min(value_step + 1, half_ring)
    for copy in table_copies:
        copy.wait_recv()
    for copy in (own_table, *own_stores):
        copy.wait()
    for group in (x_copies, y_copies, core_copies, core_x, core_y, sent, table_copies):
        for copy in group:
            copy.wait_send()


def gather(hidden, norm_gain, key_weight, value_weight, tables, dp_size, ctx_size):
    rows, width = hidden.shape
    features = key_weight.shape[1]
    pieces = 2 * PIECES
    dma = pltpu.SemaphoreType.DMA
    any_spec = pl.BlockSpec(memory_space=pl.ANY)
    return pl.pallas_call(
        functools.partial(gather_kernel, ctx_size),
        out_shape=(
            jax.ShapeDtypeStruct((ctx_size, 2, rows, features), jnp.bfloat16),
            jax.ShapeDtypeStruct(tables.shape, jnp.int32),
        ),
        in_specs=[
            any_spec,
            pl.BlockSpec(memory_space=pltpu.VMEM),
            any_spec,
            any_spec,
            any_spec,
        ],
        out_specs=(any_spec, any_spec),
        scratch_shapes=[
            pltpu.VMEM((dp_size, 2, width // dp_size, features), jnp.bfloat16),
            pltpu.VMEM((rows, width), jnp.bfloat16),
            pltpu.VMEM((rows, width), jnp.bfloat16),
            pltpu.VMEM((2, rows, features), jnp.float32),
            pltpu.VMEM((2, rows, features), jnp.bfloat16),
            dma((2, pieces)),
            dma((2, pieces)),
            dma((2, pieces)),
            dma((2, pieces)),
            dma((2, pieces)),
            dma((2, 2, 2, ctx_size // 2)),
            dma((2, ctx_size)),
            dma((pieces + 4,)),
        ],
        compiler_params=pltpu.CompilerParams(
            collective_id=0, has_side_effects=True, vmem_limit_bytes=48 * 2**20
        ),
    )(hidden, norm_gain, key_weight, value_weight, tables)


def on_device(hidden, norm_gain, queries, key_weight, value_weight, block_lists, block_counts):
    dp_size, ctx_size = lax.axis_size("dp"), lax.axis_size("ctx")
    tables = jnp.concatenate([block_lists[0], block_counts[0][..., None]], axis=-1)
    heads_each, blocks, used = tables.shape
    local_blocks = blocks // ctx_size
    tables = tables.reshape(heads_each, ctx_size, local_blocks, used).swapaxes(0, 1)
    tables = tables.reshape(ctx_size, heads_each * local_blocks, used)
    tables = jnp.pad(tables, ((0, 0), (0, 0), (0, HD - used)))
    pairs, lists = gather(
        hidden[0], norm_gain[None], key_weight, value_weight, tables, dp_size, ctx_size
    )
    return attention(lists, queries[0], pairs, heads_each * ctx_size, local_blocks)[None]


def solution(mesh):
    return jax.shard_map(
        on_device,
        mesh=mesh,
        in_specs=(
            P("dp", "ctx", None),
            P(),
            P("dp", "ctx", None),
            P("dp", None),
            P("dp", None),
            P("dp", "ctx", None, None),
            P("dp", "ctx", None),
        ),
        out_specs=P("dp", "ctx", None),
        check_vma=False,
    )
```

```python
import functools

import jax
import jax.numpy as jnp
from jax import lax
from jax.experimental import pallas as pl
from jax.experimental.pallas import tpu as pltpu
from jax.sharding import PartitionSpec as P

KVH = 4
HD = 128
BLK = 128
MAXB = 12
LOG2E = 1.4426950408889634
CHUNKS = 8
DIRECT = 5
RELAYED = CHUNKS - DIRECT
MESH = pl.DeviceIdType.MESH
BUCKETS = (2, 4, 6, 8, 10, 12)


def attention_kernel(heads, local_blocks, lists_ref, queries_ref, pairs_ref, out_ref):
    group = heads // KVH
    heads_each = heads // lists_ref.shape[0]
    factor = LOG2E * HD ** (-0.5)

    def one(head, carry):
        key_columns = pl.ds(pl.multiple_of(head // group * HD, HD), HD)
        columns = pl.ds(pl.multiple_of(head * HD, HD), HD)
        source = head // heads_each
        first = lax.rem(head, heads_each) * local_blocks
        counts = [lists_ref[source, first + block, MAXB] for block in range(local_blocks)]
        most = functools.reduce(jnp.maximum, counts)

        def gathered(which, places):
            return jnp.concatenate(
                [pairs_ref[owner, which, place, key_columns] for owner, place in places], axis=0
            )

        def attend(slots):
            row = lax.broadcasted_iota(jnp.int32, (BLK, BLK), 0)
            column = lax.broadcasted_iota(jnp.int32, (BLK, BLK), 1)
            places, scores, weights, totals = [], [], [], []
            for block in range(local_blocks):
                chosen = [lists_ref[source, first + block, s] for s in range(slots)]
                places.append(
                    [
                        (
                            pick // local_blocks,
                            pl.ds(pl.multiple_of(lax.rem(pick, local_blocks) * BLK, BLK), BLK),
                        )
                        for pick in chosen
                    ]
                )
                scores.append(
                    lax.dot_general(
                        queries_ref[block * BLK : (block + 1) * BLK, columns],
                        gathered(0, places[block]),
                        (((1,), (1,)), ((), ())),
                        preferred_element_type=jnp.float32,
                    )
                )
            for block in range(local_blocks):
                tiles = [scores[block][:, s * BLK : (s + 1) * BLK] for s in range(slots)]
                tiles[0] = jnp.where(column <= row, tiles[0], -jnp.inf)
                for s in range(1, slots):
                    tiles[s] = jnp.where(s < counts[block], tiles[s], -jnp.inf)
                peak = functools.reduce(jnp.maximum, tiles)
                peak = jnp.max(peak, axis=1, keepdims=True)
                tiles = [jnp.exp2((tile - peak) * factor) for tile in tiles]
                totals.append(jnp.sum(functools.reduce(jnp.add, tiles), axis=1, keepdims=True))
                weights.append(
                    jnp.concatenate([tile.astype(jnp.bfloat16) for tile in tiles], axis=1)
                )
            for block in range(local_blocks):
                attended = jnp.dot(
                    weights[block],
                    gathered(1, places[block]),
                    preferred_element_type=jnp.float32,
                )
                out_ref[block * BLK : (block + 1) * BLK, columns] = (
                    attended / totals[block]
                ).astype(jnp.bfloat16)

        below = 0
        for slots in BUCKETS:

            @pl.when((most > below) & (most <= slots))
            def _(slots=slots):
                attend(slots)

            below = slots
        return carry

    lax.fori_loop(0, heads, one, 0)


def attention(lists, queries, pairs, heads, local_blocks):
    return pl.pallas_call(
        functools.partial(attention_kernel, heads, local_blocks),
        out_shape=jax.ShapeDtypeStruct(queries.shape, jnp.bfloat16),
        in_specs=[
            pl.BlockSpec(memory_space=pltpu.SMEM),
            pl.BlockSpec(memory_space=pltpu.VMEM),
            pl.BlockSpec(memory_space=pltpu.VMEM),
        ],
        out_specs=pl.BlockSpec(memory_space=pltpu.VMEM),
        compiler_params=pltpu.CompilerParams(vmem_limit_bytes=48 * 2**20),
    )(lists, queries, pairs)


def gather_kernel(
    ctx_size,
    hidden_ref,
    gain_ref,
    key_ref,
    value_ref,
    table_ref,
    pairs_ref,
    tables_ref,
    weights,
    rows_in,
    normed,
    totals,
    own_pair,
    x_sems,
    y_sems,
    core_sems,
    core_x_sems,
    core_y_sems,
    ring_sems,
    table_sems,
    local_sems,
):
    dp = lax.axis_index("dp")
    ctx = lax.axis_index("ctx")
    core = dp % 2
    core_peer = dp + 1 - 2 * core
    x_peer = dp + 2 - 4 * (dp // 2)
    cross_peer = x_peer + 1 - 2 * core
    side = ctx % 2
    y_peer = ctx + 1 - 2 * side
    half_ring = ctx_size // 2
    position = (1 - side) * (ctx // 2) + side * (ctx_size - 1 - ctx // 2)

    def ctx_at(place):
        place = (place + ctx_size) % ctx_size
        second = place // half_ring
        return (1 - second) * 2 * place + second * (2 * (ctx_size - 1 - place) + 1)

    shard = key_ref.shape[0]
    chunk = shard // CHUNKS
    sources = (key_ref, value_ref)
    total_pieces = 2 * DIRECT

    barrier = pltpu.get_barrier_semaphore()
    for step in range(1, ctx_size):
        pl.semaphore_signal(
            barrier, inc=1, device_id={"ctx": (ctx + step) % ctx_size}, device_id_type=MESH
        )
    for peer in (core_peer, x_peer):
        pl.semaphore_signal(barrier, inc=1, device_id={"dp": peer}, device_id_type=MESH)
    pl.semaphore_wait(barrier, ctx_size + 1)

    def remote(src, dst, sems, index, device):
        return pltpu.make_async_remote_copy(
            src_ref=src,
            dst_ref=dst,
            send_sem=sems.at[(0, *index)],
            recv_sem=sems.at[(1, *index)],
            device_id=device,
            device_id_type=MESH,
        )

    def start_of(which, m):
        return (m + which * (CHUNKS - 1 - 2 * m)) * chunk

    def rows_of(which, m):
        return pl.ds(pl.multiple_of(start_of(which, m), chunk), chunk)

    def is_relayed(k):
        return k % DIRECT < RELAYED

    quarter_size = shard // 4
    x_copies, y_copies, core_copies, core_x, core_y, own_copies = [], {}, [], [], {}, []
    for k in range(8):
        j = k // 4
        quarter = pl.ds((k % 4) * quarter_size, quarter_size)
        core_copies.append(
            remote(
                sources[j].at[quarter],
                weights.at[dp, j, quarter],
                core_sems,
                (k,),
                {"dp": core_peer},
            )
        )
        own_copies.append(
            pltpu.make_async_copy(
                sources[j].at[quarter], weights.at[dp, j, quarter], local_sems.at[k]
            )
        )
    for k in range(total_pieces):
        j = k // DIRECT
        mine, other = rows_of(side, k % DIRECT), rows_of(1 - side, k % DIRECT)
        x_copies.append(
            remote(sources[j].at[mine], weights.at[dp, j, mine], x_sems, (k,), {"dp": x_peer})
        )
        arrived = weights.at[x_peer, j, mine]
        core_x.append(remote(arrived, arrived, core_x_sems, (k,), {"dp": core_peer}))
        if is_relayed(k):
            y_copies[k] = remote(arrived, arrived, y_sems, (k,), {"ctx": y_peer})
            second = weights.at[x_peer, j, other]
            core_y[k] = remote(second, second, core_y_sems, (k,), {"dp": core_peer})

    load = pltpu.make_async_copy(hidden_ref, rows_in, local_sems.at[8])
    load.start()
    for k in range(total_pieces):
        x_copies[k].start()
    for k in range(8):
        core_copies[k].start()
        own_copies[k].start()
    own_table = pltpu.make_async_copy(
        table_ref.at[ctx], tables_ref.at[ctx], local_sems.at[8 + 1]
    )
    own_table.start()
    table_copies = []
    for step in range(1, ctx_size):
        to = (ctx + step) % ctx_size
        table_copies.append(
            remote(table_ref.at[to], tables_ref.at[ctx], table_sems, (step,), {"ctx": to})
        )
        table_copies[-1].start()

    totals[...] = jnp.zeros_like(totals)
    load.wait()
    strip = 16

    @pl.loop(0, rows_in.shape[0] // strip)
    def _(index):
        rows = pl.ds(pl.multiple_of(index * strip, strip), strip)
        upcast = rows_in[rows, :].astype(jnp.float32)
        mean_square = jnp.mean(upcast * upcast, axis=-1, keepdims=True)
        gain = gain_ref[...].astype(jnp.float32)
        normed[rows, :] = (upcast * lax.rsqrt(mean_square + 1e-05) * gain).astype(jnp.bfloat16)

    def accumulate(owner, j, start, size):
        columns = pl.ds(pl.multiple_of(owner * shard + start, chunk), size)
        totals[j] += jnp.dot(
            normed[:, columns],
            weights[owner, j, pl.ds(pl.multiple_of(start, chunk), size), :],
            preferred_element_type=jnp.float32,
        )

    def ring_copy(j, way, step):
        sign = 1 - 2 * way
        origin = ctx_at(position - sign * step)
        source = own_pair.at[j] if step == 0 else pairs_ref.at[origin, j]
        return remote(
            source,
            pairs_ref.at[origin, j],
            ring_sems,
            (j, way, step),
            {"ctx": ctx_at(position + sign)},
        )

    def hops(j, way):
        return half_ring if j == way else half_ring - 1

    sent, own_stores = [], []

    def ring_start(j, step):
        for way in range(2):
            if step < hops(j, way):
                copy = ring_copy(j, way, step)
                copy.start()
                sent.append(copy)

    def ring_wait(j, step):
        for way in range(2):
            if step < hops(j, way):
                ring_copy(j, way, step).wait_recv()

    def finish(j):
        own_pair[j] = totals[j].astype(jnp.bfloat16)
        store = pltpu.make_async_copy(
            own_pair.at[j], pairs_ref.at[ctx, j], local_sems.at[8 + 2 + j]
        )
        store.start()
        own_stores.append(store)
        ring_start(j, 0)

    key_step = 0
    for k in range(total_pieces + 1):
        if k < total_pieces:
            x_copies[k].wait_recv()
            if is_relayed(k):
                y_copies[k].start()
            core_x[k].start()
        if k - 1 in y_copies:
            y_copies[k - 1].wait_recv()
            core_y[k - 1].start()
        if k < total_pieces:
            j, m = k // DIRECT, k % DIRECT
            if m < 4:
                quarter = 4 * j + m
                own_copies[quarter].wait()
                accumulate(dp, j, m * quarter_size, quarter_size)
                core_copies[quarter].wait_recv()
                accumulate(core_peer, j, m * quarter_size, quarter_size)
            accumulate(x_peer, j, start_of(side, m), chunk)
        if 1 <= k <= total_pieces:
            j, m = (k - 1) // DIRECT, (k - 1) % DIRECT
            if is_relayed(k - 1):
                accumulate(x_peer, j, start_of(1 - side, m), chunk)
            core_x[k - 1].wait_recv()
            accumulate(cross_peer, j, start_of(side, m), chunk)
        if k - 2 in core_y:
            j, m = (k - 2) // DIRECT, (k - 2) % DIRECT
            core_y[k - 2].wait_recv()
            accumulate(cross_peer, j, start_of(1 - side, m), chunk)
        if k == DIRECT:
            finish(0)
        if k > DIRECT and key_step < half_ring - 1:
            ring_wait(0, key_step)
            key_step += 1
            ring_start(0, key_step)
    finish(1)
    value_step = 0
    while key_step < half_ring or value_step < half_ring:
        for j, step in ((0, key_step), (1, value_step)):
            if step < half_ring:
                ring_wait(j, step)
                if step + 1 < half_ring:
                    ring_start(j, step + 1)
        key_step, value_step = min(key_step + 1, half_ring), min(value_step + 1, half_ring)
    for copy in table_copies:
        copy.wait_recv()
    for copy in (own_table, *own_stores):
        copy.wait()
    for group in (
        x_copies,
        y_copies.values(),
        core_copies,
        core_x,
        core_y.values(),
        sent,
        table_copies,
    ):
        for copy in group:
            copy.wait_send()


def gather(hidden, norm_gain, key_weight, value_weight, tables, dp_size, ctx_size):
    rows, width = hidden.shape
    features = key_weight.shape[1]
    pieces = 2 * DIRECT
    dma = pltpu.SemaphoreType.DMA
    any_spec = pl.BlockSpec(memory_space=pl.ANY)
    return pl.pallas_call(
        functools.partial(gather_kernel, ctx_size),
        out_shape=(
            jax.ShapeDtypeStruct((ctx_size, 2, rows, features), jnp.bfloat16),
            jax.ShapeDtypeStruct(tables.shape, jnp.int32),
        ),
        in_specs=[
            any_spec,
            pl.BlockSpec(memory_space=pltpu.VMEM),
            any_spec,
            any_spec,
            any_spec,
        ],
        out_specs=(any_spec, any_spec),
        scratch_shapes=[
            pltpu.VMEM((dp_size, 2, width // dp_size, features), jnp.bfloat16),
            pltpu.VMEM((rows, width), jnp.bfloat16),
            pltpu.VMEM((rows, width), jnp.bfloat16),
            pltpu.VMEM((2, rows, features), jnp.float32),
            pltpu.VMEM((2, rows, features), jnp.bfloat16),
            dma((2, pieces)),
            dma((2, pieces)),
            dma((2, 8)),
            dma((2, pieces)),
            dma((2, pieces)),
            dma((2, 2, 2, ctx_size // 2)),
            dma((2, ctx_size)),
            dma((12,)),
        ],
        compiler_params=pltpu.CompilerParams(
            collective_id=0, has_side_effects=True, vmem_limit_bytes=62 * 2**20
        ),
    )(hidden, norm_gain, key_weight, value_weight, tables)


def on_device(hidden, norm_gain, queries, key_weight, value_weight, block_lists, block_counts):
    dp_size, ctx_size = lax.axis_size("dp"), lax.axis_size("ctx")
    tables = jnp.concatenate([block_lists[0], block_counts[0][..., None]], axis=-1)
    heads_each, blocks, used = tables.shape
    local_blocks = blocks // ctx_size
    tables = tables.reshape(heads_each, ctx_size, local_blocks, used).swapaxes(0, 1)
    tables = tables.reshape(ctx_size, heads_each * local_blocks, used)
    tables = jnp.pad(tables, ((0, 0), (0, 0), (0, HD - used)))
    pairs, lists = gather(
        hidden[0], norm_gain[None], key_weight, value_weight, tables, dp_size, ctx_size
    )
    return attention(lists, queries[0], pairs, heads_each * ctx_size, local_blocks)[None]


def solution(mesh):
    return jax.shard_map(
        on_device,
        mesh=mesh,
        in_specs=(
            P("dp", "ctx", None),
            P(),
            P("dp", "ctx", None),
            P("dp", None),
            P("dp", None),
            P("dp", "ctx", None, None),
            P("dp", "ctx", None),
        ),
        out_specs=P("dp", "ctx", None),
        check_vma=False,
    )
```

```python
import functools

import jax
import jax.numpy as jnp
from jax import lax
from jax.experimental import pallas as pl
from jax.experimental.pallas import tpu as pltpu
from jax.sharding import PartitionSpec as P

KVH = 4
HD = 128
BLK = 128
MAXB = 12
LOG2E = 1.4426950408889634
PARTS = 4
CHUNKS = 8
DIRECT = 5
RELAYED = CHUNKS - DIRECT
MESH = pl.DeviceIdType.MESH
BUCKETS = (2, 4, 6, 8, 10, 12)


def attention_kernel(heads, local_blocks, lists_ref, queries_ref, keys_ref, values_ref, out_ref):
    group = heads // KVH
    first_head = pl.program_id(0) * group
    heads_each = heads // lists_ref.shape[0]
    factor = LOG2E * HD ** (-0.5)

    def one(step, carry):
        head = first_head + step
        columns = pl.ds(pl.multiple_of(step * HD, HD), HD)
        source = head // heads_each
        first = lax.rem(head, heads_each) * local_blocks
        counts = [lists_ref[source, first + block, MAXB] for block in range(local_blocks)]
        most = functools.reduce(jnp.maximum, counts)

        def gathered(ref, places):
            return jnp.concatenate(
                [ref[owner, 0, place, :] for owner, place in places], axis=0
            )

        def attend(slots):
            row = lax.broadcasted_iota(jnp.int32, (BLK, BLK), 0)
            column = lax.broadcasted_iota(jnp.int32, (BLK, BLK), 1)
            places, scores, weights, totals = [], [], [], []
            for block in range(local_blocks):
                chosen = [lists_ref[source, first + block, s] for s in range(slots)]
                places.append(
                    [
                        (
                            pick // local_blocks,
                            pl.ds(pl.multiple_of(lax.rem(pick, local_blocks) * BLK, BLK), BLK),
                        )
                        for pick in chosen
                    ]
                )
                scores.append(
                    lax.dot_general(
                        queries_ref[block * BLK : (block + 1) * BLK, columns],
                        gathered(keys_ref, places[block]),
                        (((1,), (1,)), ((), ())),
                        preferred_element_type=jnp.float32,
                    )
                )
            for block in range(local_blocks):
                tiles = [scores[block][:, s * BLK : (s + 1) * BLK] for s in range(slots)]
                tiles[0] = jnp.where(column <= row, tiles[0], -jnp.inf)
                for s in range(1, slots):
                    tiles[s] = jnp.where(s < counts[block], tiles[s], -jnp.inf)
                peak = functools.reduce(jnp.maximum, tiles)
                peak = jnp.max(peak, axis=1, keepdims=True)
                tiles = [jnp.exp2((tile - peak) * factor) for tile in tiles]
                totals.append(jnp.sum(functools.reduce(jnp.add, tiles), axis=1, keepdims=True))
                weights.append(
                    jnp.concatenate([tile.astype(jnp.bfloat16) for tile in tiles], axis=1)
                )
            for block in range(local_blocks):
                attended = jnp.dot(
                    weights[block],
                    gathered(values_ref, places[block]),
                    preferred_element_type=jnp.float32,
                )
                out_ref[block * BLK : (block + 1) * BLK, columns] = (
                    attended / totals[block]
                ).astype(jnp.bfloat16)

        below = 0
        for slots in BUCKETS:

            @pl.when((most > below) & (most <= slots))
            def _(slots=slots):
                attend(slots)

            below = slots
        return carry

    lax.fori_loop(0, group, one, 0)


def attention(lists, queries, pairs, heads, local_blocks):
    rows, width = queries.shape
    per_part = PARTS // 2
    shared = KVH // per_part
    wide = pl.BlockSpec((rows, width // KVH), lambda g: (0, g))
    block = (pairs.shape[0], 1, rows, HD)
    return pl.pallas_call(
        functools.partial(attention_kernel, heads, local_blocks),
        grid=(KVH,),
        out_shape=jax.ShapeDtypeStruct(queries.shape, jnp.bfloat16),
        in_specs=[
            pl.BlockSpec(memory_space=pltpu.SMEM),
            wide,
            pl.BlockSpec(block, lambda g: (0, g // shared, 0, g % shared)),
            pl.BlockSpec(block, lambda g: (0, per_part + g // shared, 0, g % shared)),
        ],
        out_specs=wide,
        compiler_params=pltpu.CompilerParams(vmem_limit_bytes=62 * 2**20),
    )(lists, queries, pairs, pairs)


def gather_kernel(
    ctx_size,
    hidden_ref,
    gain_ref,
    key_ref,
    value_ref,
    table_ref,
    pairs_ref,
    tables_ref,
    weights,
    rows_in,
    normed,
    totals,
    own_pair,
    x_sems,
    y_sems,
    core_sems,
    core_x_sems,
    core_y_sems,
    ring_sems,
    table_sems,
    local_sems,
):
    dp = lax.axis_index("dp")
    ctx = lax.axis_index("ctx")
    core = dp % 2
    core_peer = dp + 1 - 2 * core
    x_peer = dp + 2 - 4 * (dp // 2)
    cross_peer = x_peer + 1 - 2 * core
    side = ctx % 2
    y_peer = ctx + 1 - 2 * side
    half_ring = ctx_size // 2
    position = (1 - side) * (ctx // 2) + side * (ctx_size - 1 - ctx // 2)

    def ctx_at(place):
        place = (place + ctx_size) % ctx_size
        second = place // half_ring
        return (1 - second) * 2 * place + second * (2 * (ctx_size - 1 - place) + 1)

    shard = key_ref.shape[0]
    chunk = shard // CHUNKS
    features = key_ref.shape[1] * 2 // PARTS
    total_pieces = PARTS * DIRECT

    def source(j, rows):
        ref = (key_ref, value_ref)[j * 2 // PARTS]
        return ref.at[rows, pl.ds(j % (PARTS // 2) * features, features)]


    barrier = pltpu.get_barrier_semaphore()
    for step in range(1, ctx_size):
        pl.semaphore_signal(
            barrier, inc=1, device_id={"ctx": (ctx + step) % ctx_size}, device_id_type=MESH
        )
    for peer in (core_peer, x_peer):
        pl.semaphore_signal(barrier, inc=1, device_id={"dp": peer}, device_id_type=MESH)
    pl.semaphore_wait(barrier, ctx_size + 1)

    def remote(src, dst, sems, index, device):
        return pltpu.make_async_remote_copy(
            src_ref=src,
            dst_ref=dst,
            send_sem=sems.at[(0, *index)],
            recv_sem=sems.at[(1, *index)],
            device_id=device,
            device_id_type=MESH,
        )

    def start_of(which, m):
        return (m + which * (CHUNKS - 1 - 2 * m)) * chunk

    def rows_of(which, m):
        return pl.ds(pl.multiple_of(start_of(which, m), chunk), chunk)

    def is_relayed(k):
        return k % DIRECT < RELAYED

    quarter_size = shard // 4
    x_copies, y_copies, core_copies, core_x, core_y, own_copies = [], {}, [], [], {}, []
    for k in range(4 * PARTS):
        j = k // 4
        quarter = pl.ds((k % 4) * quarter_size, quarter_size)
        core_copies.append(
            remote(
                source(j, quarter),
                weights.at[dp, j, quarter],
                core_sems,
                (k,),
                {"dp": core_peer},
            )
        )
        own_copies.append(
            pltpu.make_async_copy(
                source(j, quarter), weights.at[dp, j, quarter], local_sems.at[k]
            )
        )
    for k in range(total_pieces):
        j = k // DIRECT
        mine, other = rows_of(side, k % DIRECT), rows_of(1 - side, k % DIRECT)
        x_copies.append(
            remote(source(j, mine), weights.at[dp, j, mine], x_sems, (k,), {"dp": x_peer})
        )
        arrived = weights.at[x_peer, j, mine]
        core_x.append(remote(arrived, arrived, core_x_sems, (k,), {"dp": core_peer}))
        if is_relayed(k):
            y_copies[k] = remote(arrived, arrived, y_sems, (k,), {"ctx": y_peer})
            second = weights.at[x_peer, j, other]
            core_y[k] = remote(second, second, core_y_sems, (k,), {"dp": core_peer})

    load = pltpu.make_async_copy(hidden_ref, rows_in, local_sems.at[4 * PARTS])
    load.start()
    for k in range(total_pieces):
        x_copies[k].start()
    for k in range(4 * PARTS):
        core_copies[k].start()
        own_copies[k].start()
    own_table = pltpu.make_async_copy(
        table_ref.at[ctx], tables_ref.at[ctx], local_sems.at[4 * PARTS + 1]
    )
    own_table.start()
    table_copies = []
    for step in range(1, ctx_size):
        to = (ctx + step) % ctx_size
        table_copies.append(
            remote(table_ref.at[to], tables_ref.at[ctx], table_sems, (step,), {"ctx": to})
        )
        table_copies[-1].start()

    totals[...] = jnp.zeros_like(totals)
    load.wait()
    strip = 16

    @pl.loop(0, rows_in.shape[0] // strip)
    def _(index):
        rows = pl.ds(pl.multiple_of(index * strip, strip), strip)
        upcast = rows_in[rows, :].astype(jnp.float32)
        mean_square = jnp.mean(upcast * upcast, axis=-1, keepdims=True)
        gain = gain_ref[...].astype(jnp.float32)
        normed[rows, :] = (upcast * lax.rsqrt(mean_square + 1e-05) * gain).astype(jnp.bfloat16)

    def accumulate(owner, j, start, size):
        columns = pl.ds(pl.multiple_of(owner * shard + start, chunk), size)
        totals[j] += jnp.dot(
            normed[:, columns],
            weights[owner, j, pl.ds(pl.multiple_of(start, chunk), size), :],
            preferred_element_type=jnp.float32,
        )

    def ring_copy(j, way, step):
        sign = 1 - 2 * way
        origin = ctx_at(position - sign * step)
        source = own_pair.at[j] if step == 0 else pairs_ref.at[origin, j]
        return remote(
            source,
            pairs_ref.at[origin, j],
            ring_sems,
            (j, way, step),
            {"ctx": ctx_at(position + sign)},
        )

    def hops(j, way):
        return half_ring if j % 2 == way else half_ring - 1

    sent, own_stores = [], []

    def ring_start(j, step):
        for way in range(2):
            if step < hops(j, way):
                copy = ring_copy(j, way, step)
                copy.start()
                sent.append(copy)

    def ring_wait(j, step):
        for way in range(2):
            if step < hops(j, way):
                ring_copy(j, way, step).wait_recv()

    def finish(j):
        own_pair[j] = totals[j].astype(jnp.bfloat16)
        store = pltpu.make_async_copy(
            own_pair.at[j], pairs_ref.at[ctx, j], local_sems.at[4 * PARTS + 2 + j]
        )
        store.start()
        own_stores.append(store)
        ring_start(j, 0)

    steps = {}

    def advance():
        for j in list(steps):
            ring_wait(j, steps[j])
            steps[j] += 1
            if steps[j] == half_ring:
                del steps[j]
            else:
                ring_start(j, steps[j])

    for k in range(total_pieces + 1):
        if k < total_pieces:
            x_copies[k].wait_recv()
            if is_relayed(k):
                y_copies[k].start()
            core_x[k].start()
        if k - 1 in y_copies:
            y_copies[k - 1].wait_recv()
            core_y[k - 1].start()
        if k < total_pieces:
            j, m = k // DIRECT, k % DIRECT
            if m < 4:
                quarter = 4 * j + m
                own_copies[quarter].wait()
                accumulate(dp, j, m * quarter_size, quarter_size)
                core_copies[quarter].wait_recv()
                accumulate(core_peer, j, m * quarter_size, quarter_size)
            accumulate(x_peer, j, start_of(side, m), chunk)
        if 1 <= k <= total_pieces:
            j, m = (k - 1) // DIRECT, (k - 1) % DIRECT
            if is_relayed(k - 1):
                accumulate(x_peer, j, start_of(1 - side, m), chunk)
            core_x[k - 1].wait_recv()
            accumulate(cross_peer, j, start_of(side, m), chunk)
        if k - 2 in core_y:
            j, m = (k - 2) // DIRECT, (k - 2) % DIRECT
            core_y[k - 2].wait_recv()
            accumulate(cross_peer, j, start_of(1 - side, m), chunk)
        if k > DIRECT:
            advance()
        if k and k % DIRECT == 0:
            finish(k // DIRECT - 1)
            steps[k // DIRECT - 1] = 0
    while steps:
        advance()
    for copy in table_copies:
        copy.wait_recv()
    for copy in (own_table, *own_stores):
        copy.wait()
    for group in (
        x_copies,
        y_copies.values(),
        core_copies,
        core_x,
        core_y.values(),
        sent,
        table_copies,
    ):
        for copy in group:
            copy.wait_send()


def gather(hidden, norm_gain, key_weight, value_weight, tables, dp_size, ctx_size):
    rows, width = hidden.shape
    features = key_weight.shape[1] * 2 // PARTS
    pieces = PARTS * DIRECT
    dma = pltpu.SemaphoreType.DMA
    any_spec = pl.BlockSpec(memory_space=pl.ANY)
    return pl.pallas_call(
        functools.partial(gather_kernel, ctx_size),
        out_shape=(
            jax.ShapeDtypeStruct((ctx_size, PARTS, rows, features), jnp.bfloat16),
            jax.ShapeDtypeStruct(tables.shape, jnp.int32),
        ),
        in_specs=[
            any_spec,
            pl.BlockSpec(memory_space=pltpu.VMEM),
            any_spec,
            any_spec,
            any_spec,
        ],
        out_specs=(any_spec, any_spec),
        scratch_shapes=[
            pltpu.VMEM((dp_size, PARTS, width // dp_size, features), jnp.bfloat16),
            pltpu.VMEM((rows, width), jnp.bfloat16),
            pltpu.VMEM((rows, width), jnp.bfloat16),
            pltpu.VMEM((PARTS, rows, features), jnp.float32),
            pltpu.VMEM((PARTS, rows, features), jnp.bfloat16),
            dma((2, pieces)),
            dma((2, pieces)),
            dma((2, 4 * PARTS)),
            dma((2, pieces)),
            dma((2, pieces)),
            dma((2, PARTS, 2, ctx_size // 2)),
            dma((2, ctx_size)),
            dma((5 * PARTS + 2,)),
        ],
        compiler_params=pltpu.CompilerParams(
            collective_id=0, has_side_effects=True, vmem_limit_bytes=62 * 2**20
        ),
    )(hidden, norm_gain, key_weight, value_weight, tables)


def on_device(hidden, norm_gain, queries, key_weight, value_weight, block_lists, block_counts):
    dp_size, ctx_size = lax.axis_size("dp"), lax.axis_size("ctx")
    tables = jnp.concatenate([block_lists[0], block_counts[0][..., None]], axis=-1)
    heads_each, blocks, used = tables.shape
    local_blocks = blocks // ctx_size
    tables = tables.reshape(heads_each, ctx_size, local_blocks, used).swapaxes(0, 1)
    tables = tables.reshape(ctx_size, heads_each * local_blocks, used)
    tables = jnp.pad(tables, ((0, 0), (0, 0), (0, HD - used)))
    pairs, lists = gather(
        hidden[0], norm_gain[None], key_weight, value_weight, tables, dp_size, ctx_size
    )
    return attention(lists, queries[0], pairs, heads_each * ctx_size, local_blocks)[None]


def solution(mesh):
    return jax.shard_map(
        on_device,
        mesh=mesh,
        in_specs=(
            P("dp", "ctx", None),
            P(),
            P("dp", "ctx", None),
            P("dp", None),
            P("dp", None),
            P("dp", "ctx", None, None),
            P("dp", "ctx", None),
        ),
        out_specs=P("dp", "ctx", None),
        check_vma=False,
    )
```

```python
import functools

import jax
import jax.numpy as jnp
from jax import lax
from jax.experimental import pallas as pl
from jax.experimental.pallas import tpu as pltpu
from jax.sharding import PartitionSpec as P

KVH = 4
HD = 128
BLK = 128
MAXB = 12
LOG2E = 1.4426950408889634
PARTS = 2
CHUNKS = 8
DIRECT = 5
RELAYED = CHUNKS - DIRECT
MESH = pl.DeviceIdType.MESH
BUCKETS = (2, 4, 6, 8, 10, 12)


def attention_kernel(heads, local_blocks, lists_ref, queries_ref, keys_ref, values_ref, out_ref):
    group = heads // KVH
    first_head = pl.program_id(0) * group
    heads_each = heads // lists_ref.shape[0]
    factor = LOG2E * HD ** (-0.5)

    def one(step, carry):
        head = first_head + step
        columns = pl.ds(pl.multiple_of(step * HD, HD), HD)
        source = head // heads_each
        first = lax.rem(head, heads_each) * local_blocks
        counts = [lists_ref[source, first + block, MAXB] for block in range(local_blocks)]
        most = functools.reduce(jnp.maximum, counts)

        def gathered(ref, places):
            return jnp.concatenate(
                [ref[owner, 0, place, :] for owner, place in places], axis=0
            )

        def attend(slots):
            row = lax.broadcasted_iota(jnp.int32, (BLK, BLK), 0)
            column = lax.broadcasted_iota(jnp.int32, (BLK, BLK), 1)
            places, scores, weights, totals = [], [], [], []
            for block in range(local_blocks):
                chosen = [lists_ref[source, first + block, s] for s in range(slots)]
                places.append(
                    [
                        (
                            pick // local_blocks,
                            pl.ds(pl.multiple_of(lax.rem(pick, local_blocks) * BLK, BLK), BLK),
                        )
                        for pick in chosen
                    ]
                )
                scores.append(
                    lax.dot_general(
                        queries_ref[block * BLK : (block + 1) * BLK, columns],
                        gathered(keys_ref, places[block]),
                        (((1,), (1,)), ((), ())),
                        preferred_element_type=jnp.float32,
                    )
                )
            for block in range(local_blocks):
                tiles = [scores[block][:, s * BLK : (s + 1) * BLK] for s in range(slots)]
                tiles[0] = jnp.where(column <= row, tiles[0], -jnp.inf)
                for s in range(1, slots):
                    tiles[s] = jnp.where(s < counts[block], tiles[s], -jnp.inf)
                peak = functools.reduce(jnp.maximum, tiles)
                peak = jnp.max(peak, axis=1, keepdims=True)
                tiles = [jnp.exp2((tile - peak) * factor) for tile in tiles]
                totals.append(jnp.sum(functools.reduce(jnp.add, tiles), axis=1, keepdims=True))
                weights.append(
                    jnp.concatenate([tile.astype(jnp.bfloat16) for tile in tiles], axis=1)
                )
            for block in range(local_blocks):
                attended = jnp.dot(
                    weights[block],
                    gathered(values_ref, places[block]),
                    preferred_element_type=jnp.float32,
                )
                out_ref[block * BLK : (block + 1) * BLK, columns] = (
                    attended / totals[block]
                ).astype(jnp.bfloat16)

        below = 0
        for slots in BUCKETS:

            @pl.when((most > below) & (most <= slots))
            def _(slots=slots):
                attend(slots)

            below = slots
        return carry

    lax.fori_loop(0, group, one, 0)


def attention(lists, queries, pairs, heads, local_blocks):
    rows, width = queries.shape
    per_part = PARTS // 2
    shared = KVH // per_part
    wide = pl.BlockSpec((rows, width // KVH), lambda g: (0, g))
    block = (pairs.shape[0], 1, rows, HD)
    return pl.pallas_call(
        functools.partial(attention_kernel, heads, local_blocks),
        grid=(KVH,),
        out_shape=jax.ShapeDtypeStruct(queries.shape, jnp.bfloat16),
        in_specs=[
            pl.BlockSpec(memory_space=pltpu.SMEM),
            wide,
            pl.BlockSpec(block, lambda g: (0, g // shared, 0, g % shared)),
            pl.BlockSpec(block, lambda g: (0, per_part + g // shared, 0, g % shared)),
        ],
        out_specs=wide,
        compiler_params=pltpu.CompilerParams(vmem_limit_bytes=62 * 2**20),
    )(lists, queries, pairs, pairs)


def gather_kernel(
    ctx_size,
    hidden_ref,
    gain_ref,
    key_ref,
    value_ref,
    table_ref,
    pairs_ref,
    tables_ref,
    weights,
    rows_in,
    normed,
    totals,
    own_pair,
    x_sems,
    y_sems,
    core_sems,
    core_x_sems,
    core_y_sems,
    ring_sems,
    table_sems,
    local_sems,
):
    dp = lax.axis_index("dp")
    ctx = lax.axis_index("ctx")
    core = dp % 2
    core_peer = dp + 1 - 2 * core
    x_peer = dp + 2 - 4 * (dp // 2)
    cross_peer = x_peer + 1 - 2 * core
    side = ctx % 2
    y_peer = ctx + 1 - 2 * side
    half_ring = ctx_size // 2
    position = (1 - side) * (ctx // 2) + side * (ctx_size - 1 - ctx // 2)

    def ctx_at(place):
        place = (place + ctx_size) % ctx_size
        second = place // half_ring
        return (1 - second) * 2 * place + second * (2 * (ctx_size - 1 - place) + 1)

    shard = key_ref.shape[0]
    chunk = shard // CHUNKS
    features = key_ref.shape[1] * 2 // PARTS
    total_pieces = PARTS * DIRECT

    def source(j, rows):
        ref = (key_ref, value_ref)[j * 2 // PARTS]
        return ref.at[rows, pl.ds(j % (PARTS // 2) * features, features)]


    barrier = pltpu.get_barrier_semaphore()
    for step in range(1, ctx_size):
        pl.semaphore_signal(
            barrier, inc=1, device_id={"ctx": (ctx + step) % ctx_size}, device_id_type=MESH
        )
    for peer in (core_peer, x_peer):
        pl.semaphore_signal(barrier, inc=1, device_id={"dp": peer}, device_id_type=MESH)
    pl.semaphore_wait(barrier, ctx_size + 1)

    def remote(src, dst, sems, index, device):
        return pltpu.make_async_remote_copy(
            src_ref=src,
            dst_ref=dst,
            send_sem=sems.at[(0, *index)],
            recv_sem=sems.at[(1, *index)],
            device_id=device,
            device_id_type=MESH,
        )

    def start_of(which, m):
        return (m + which * (CHUNKS - 1 - 2 * m)) * chunk

    def rows_of(which, m):
        return pl.ds(pl.multiple_of(start_of(which, m), chunk), chunk)

    def is_relayed(k):
        return k % DIRECT < RELAYED

    quarter_size = shard // 4
    x_copies, y_copies, core_copies, core_x, core_y, own_copies = [], {}, [], [], {}, []
    for k in range(4 * PARTS):
        j = k // 4
        quarter = pl.ds((k % 4) * quarter_size, quarter_size)
        core_copies.append(
            remote(
                source(j, quarter),
                weights.at[dp, j, quarter],
                core_sems,
                (k,),
                {"dp": core_peer},
            )
        )
        own_copies.append(
            pltpu.make_async_copy(
                source(j, quarter), weights.at[dp, j, quarter], local_sems.at[k]
            )
        )
    for k in range(total_pieces):
        j = k // DIRECT
        mine, other = rows_of(side, k % DIRECT), rows_of(1 - side, k % DIRECT)
        x_copies.append(
            remote(source(j, mine), weights.at[dp, j, mine], x_sems, (k,), {"dp": x_peer})
        )
        arrived = weights.at[x_peer, j, mine]
        core_x.append(remote(arrived, arrived, core_x_sems, (k,), {"dp": core_peer}))
        if is_relayed(k):
            y_copies[k] = remote(arrived, arrived, y_sems, (k,), {"ctx": y_peer})
            second = weights.at[x_peer, j, other]
            core_y[k] = remote(second, second, core_y_sems, (k,), {"dp": core_peer})

    load = pltpu.make_async_copy(hidden_ref, rows_in, local_sems.at[4 * PARTS])
    load.start()
    for k in range(total_pieces):
        x_copies[k].start()
    for k in range(4 * PARTS):
        core_copies[k].start()
        own_copies[k].start()
    own_table = pltpu.make_async_copy(
        table_ref.at[ctx], tables_ref.at[ctx], local_sems.at[4 * PARTS + 1]
    )
    own_table.start()
    table_copies = []
    for step in range(1, ctx_size):
        to = (ctx + step) % ctx_size
        table_copies.append(
            remote(table_ref.at[to], tables_ref.at[ctx], table_sems, (step,), {"ctx": to})
        )
        table_copies[-1].start()

    totals[...] = jnp.zeros_like(totals)
    load.wait()
    strip = 16

    @pl.loop(0, rows_in.shape[0] // strip)
    def _(index):
        rows = pl.ds(pl.multiple_of(index * strip, strip), strip)
        upcast = rows_in[rows, :].astype(jnp.float32)
        mean_square = jnp.mean(upcast * upcast, axis=-1, keepdims=True)
        gain = gain_ref[...].astype(jnp.float32)
        normed[rows, :] = (upcast * lax.rsqrt(mean_square + 1e-05) * gain).astype(jnp.bfloat16)

    def accumulate(owner, j, start, size):
        columns = pl.ds(pl.multiple_of(owner * shard + start, chunk), size)
        totals[j] += jnp.dot(
            normed[:, columns],
            weights[owner, j, pl.ds(pl.multiple_of(start, chunk), size), :],
            preferred_element_type=jnp.float32,
        )

    def ring_copy(j, way, step):
        sign = 1 - 2 * way
        origin = ctx_at(position - sign * step)
        source = own_pair.at[j] if step == 0 else pairs_ref.at[origin, j]
        return remote(
            source,
            pairs_ref.at[origin, j],
            ring_sems,
            (j, way, step),
            {"ctx": ctx_at(position + sign)},
        )

    def hops(j, way):
        return half_ring if j % 2 == way else half_ring - 1

    sent, own_stores = [], []

    def ring_start(j, step):
        for way in range(2):
            if step < hops(j, way):
                copy = ring_copy(j, way, step)
                copy.start()
                sent.append(copy)

    def ring_wait(j, step):
        for way in range(2):
            if step < hops(j, way):
                ring_copy(j, way, step).wait_recv()

    def finish(j):
        own_pair[j] = totals[j].astype(jnp.bfloat16)
        store = pltpu.make_async_copy(
            own_pair.at[j], pairs_ref.at[ctx, j], local_sems.at[4 * PARTS + 2 + j]
        )
        store.start()
        own_stores.append(store)
        ring_start(j, 0)

    steps = {}

    def advance():
        for j in list(steps):
            ring_wait(j, steps[j])
            steps[j] += 1
            if steps[j] == half_ring:
                del steps[j]
            else:
                ring_start(j, steps[j])

    for k in range(total_pieces + 1):
        if k < total_pieces:
            x_copies[k].wait_recv()
            if is_relayed(k):
                y_copies[k].start()
            core_x[k].start()
        if k - 1 in y_copies:
            y_copies[k - 1].wait_recv()
            core_y[k - 1].start()
        if k < total_pieces:
            j, m = k // DIRECT, k % DIRECT
            if m < 4:
                quarter = 4 * j + m
                own_copies[quarter].wait()
                accumulate(dp, j, m * quarter_size, quarter_size)
                core_copies[quarter].wait_recv()
                accumulate(core_peer, j, m * quarter_size, quarter_size)
            accumulate(x_peer, j, start_of(side, m), chunk)
        if 1 <= k <= total_pieces:
            j, m = (k - 1) // DIRECT, (k - 1) % DIRECT
            if is_relayed(k - 1):
                accumulate(x_peer, j, start_of(1 - side, m), chunk)
            core_x[k - 1].wait_recv()
            accumulate(cross_peer, j, start_of(side, m), chunk)
        if k - 2 in core_y:
            j, m = (k - 2) // DIRECT, (k - 2) % DIRECT
            core_y[k - 2].wait_recv()
            accumulate(cross_peer, j, start_of(1 - side, m), chunk)
        if k > DIRECT:
            advance()
        if k and k % DIRECT == 0:
            finish(k // DIRECT - 1)
            steps[k // DIRECT - 1] = 0
    while steps:
        advance()
    for copy in table_copies:
        copy.wait_recv()
    for copy in (own_table, *own_stores):
        copy.wait()
    for group in (
        x_copies,
        y_copies.values(),
        core_copies,
        core_x,
        core_y.values(),
        sent,
        table_copies,
    ):
        for copy in group:
            copy.wait_send()


def gather(hidden, norm_gain, key_weight, value_weight, tables, dp_size, ctx_size):
    rows, width = hidden.shape
    features = key_weight.shape[1] * 2 // PARTS
    pieces = PARTS * DIRECT
    dma = pltpu.SemaphoreType.DMA
    any_spec = pl.BlockSpec(memory_space=pl.ANY)
    return pl.pallas_call(
        functools.partial(gather_kernel, ctx_size),
        out_shape=(
            jax.ShapeDtypeStruct((ctx_size, PARTS, rows, features), jnp.bfloat16),
            jax.ShapeDtypeStruct(tables.shape, jnp.int32),
        ),
        in_specs=[
            any_spec,
            pl.BlockSpec(memory_space=pltpu.VMEM),
            any_spec,
            any_spec,
            any_spec,
        ],
        out_specs=(any_spec, any_spec),
        scratch_shapes=[
            pltpu.VMEM((dp_size, PARTS, width // dp_size, features), jnp.bfloat16),
            pltpu.VMEM((rows, width), jnp.bfloat16),
            pltpu.VMEM((rows, width), jnp.bfloat16),
            pltpu.VMEM((PARTS, rows, features), jnp.float32),
            pltpu.VMEM((PARTS, rows, features), jnp.bfloat16),
            dma((2, pieces)),
            dma((2, pieces)),
            dma((2, 4 * PARTS)),
            dma((2, pieces)),
            dma((2, pieces)),
            dma((2, PARTS, 2, ctx_size // 2)),
            dma((2, ctx_size)),
            dma((5 * PARTS + 2,)),
        ],
        compiler_params=pltpu.CompilerParams(
            collective_id=0, has_side_effects=True, vmem_limit_bytes=62 * 2**20
        ),
    )(hidden, norm_gain, key_weight, value_weight, tables)


def on_device(hidden, norm_gain, queries, key_weight, value_weight, block_lists, block_counts):
    dp_size, ctx_size = lax.axis_size("dp"), lax.axis_size("ctx")
    tables = jnp.concatenate([block_lists[0], block_counts[0][..., None]], axis=-1)
    heads_each, blocks, used = tables.shape
    local_blocks = blocks // ctx_size
    tables = tables.reshape(heads_each, ctx_size, local_blocks, used).swapaxes(0, 1)
    tables = tables.reshape(ctx_size, heads_each * local_blocks, used)
    tables = jnp.pad(tables, ((0, 0), (0, 0), (0, HD - used)))
    pairs, lists = gather(
        hidden[0], norm_gain[None], key_weight, value_weight, tables, dp_size, ctx_size
    )
    return attention(lists, queries[0], pairs, heads_each * ctx_size, local_blocks)[None]


def solution(mesh):
    return jax.shard_map(
        on_device,
        mesh=mesh,
        in_specs=(
            P("dp", "ctx", None),
            P(),
            P("dp", "ctx", None),
            P("dp", None),
            P("dp", None),
            P("dp", "ctx", None, None),
            P("dp", "ctx", None),
        ),
        out_specs=P("dp", "ctx", None),
        check_vma=False,
    )
```
